256 devices in a mesh: blk: 32 (over y_hi, z, core), uly: 8 (over x, y_lo).
Axes of the slice: x: 4, y: 4 (y_hi: 2, y_lo: 2; y = y_hi * 2 + y_lo), z: 8, core: 2. Of those that a mesh axis runs over, the one named last changes fastest.
Arguments:
- query_rows: bfloat16 [65536, 1024], P(('blk', 'uly')), may hold values from -6 to 6
- key_rows: bfloat16 [65536, 128], P('blk'), may hold values from -6 to 6
- value_rows: bfloat16 [65536, 128], P('blk'), may hold values from -6 to 6
- forward_output: bfloat16 [65536, 1024], P('blk', 'uly'), may hold values from -6 to 6
- grad_output: bfloat16 [65536, 1024], P(('blk', 'uly')), may hold values from -48 to 48
- log_normalizer: float32 [8, 65536], P('uly', 'blk'), may hold values from 1 to 9
- block_order: int32 [64], replicated, may hold values from 0 to 63, as said below
- block_table: int32 [64, 64], replicated, may hold values 0 or 1
Outputs:
- grad_query: bfloat16 [65536, 1024], P(('blk', 'uly'))
- grad_key: bfloat16 [65536, 128], P(('blk', 'uly'))
- grad_value: bfloat16 [65536, 128], P(('blk', 'uly'))
The draws below stay inside these ranges and needn't reach their ends.
Inputs may be any that keep to these rules, and one draw needn't show every extreme that they name: `block_order`: stored blocks 2 i and 2 i + 1 hold sequence blocks b and 63 - b for some b; each of 0 to 63 appears once.
All inputs are finite; a program needn't handle non-finite values.
Results may differ from the reference program's by a relative error of at most 0.0065.
Values may be sent and summed in bfloat16 or wider, within the bound.
A program may use at most 128 MiB of HBM per device.

```python
import math
import jax
import jax.numpy as jnp
from jax import lax

H = 8
DH = 128
BLK_ROWS = 1024
CYCLE_STEPS = 2
BLOCKS = 64
TOKENS = 65536
N_BLK = 32


def draw_block_order(key, part):
    key = jax.random.fold_in(key, 1)
    first_half = jax.random.permutation(key, BLOCKS // 2).astype(jnp.int32)
    paired = jnp.stack([first_half, BLOCKS - 1 - first_half], axis=1)
    return paired.reshape(BLOCKS).astype(jnp.int32)


def draw_log_normalizer(key, part):
    key = jax.random.fold_in(key, 2)
    row_index = jnp.arange(TOKENS, dtype=jnp.int32)
    centre = jnp.log((row_index % BLK_ROWS).astype(jnp.float32) + 1.0 + BLK_ROWS)
    spread = jax.random.uniform(key, (H, TOKENS), jnp.float32, -0.5, 0.5)
    return (centre[None, :] + spread).astype(jnp.float32)


def set_ends(entries, rng, low, largest):
    extent = entries.shape
    place = [jax.random.randint(jax.random.fold_in(rng, axis), (), 0, extent[axis]) for axis in range(len(extent))]
    entries = entries.at[tuple(place)].set(low)
    longest = extent.index(max(extent))
    place[longest] = (place[longest] + 1) % extent[longest]
    return entries.at[tuple(place)].set(largest)


def levels(key, shape, shards, smallest, top_value):
    loudness, own = 1.0, jax.random.fold_in(key, 6)
    for dim, parts in shards:
        draws = jnp.exp(jax.random.uniform(jax.random.fold_in(own, dim), (parts,), jnp.float32, smallest / len(shards), top_value / len(shards)))
        loudness = loudness * jnp.repeat(draws, shape[dim] // parts).reshape([-1 if axis == dim else 1 for axis in range(len(shape))])
    return loudness


def normal_values(rng, extent, scale, bound, pieces=(), held_as=jnp.bfloat16):
    array = jax.random.normal(rng, extent, jnp.float32) * scale
    if len(pieces) > 0:
        array = levels(rng, extent, pieces, -0.22, 0.18) * array
    return jnp.clip(array, min=-bound, max=bound).astype(held_as)


def setup_inputs(seed: int = 0) -> dict:
    seeds = jax.random.split(jax.random.key(seed), 9)
    query_rows = normal_values(seeds[0], (TOKENS, H * DH), 1.0, 6.0, ((0, 256),))
    key_rows = normal_values(seeds[1], (TOKENS, DH), 1.0, 6.0, ((0, 32),))
    value_rows = normal_values(seeds[2], (TOKENS, DH), 1.0, 6.0, ((0, 32),))
    forward_output = normal_values(seeds[3], (TOKENS, H * DH), 1.0, 6.0, ((0, 32), (1, 8)))
    grad_output = normal_values(seeds[4], (TOKENS, H * DH), 8.0, 48.0, ((0, 256),))
    log_normalizer = draw_log_normalizer(jax.random.fold_in(seeds[8], 71), 0)
    block_order = draw_block_order(jax.random.fold_in(seeds[8], 71), 0)
    block_table = set_ends((jax.random.randint(seeds[7], (BLOCKS, BLOCKS), 0, 4) < 3).astype(jnp.int32), jax.random.fold_in(seeds[7], 1), 0, 1)
    return {"query_rows": query_rows, "key_rows": key_rows, "value_rows": value_rows, "forward_output": forward_output, "grad_output": grad_output, "log_normalizer": log_normalizer, "block_order": block_order, "block_table": block_table}


def round_half(values):
    lowered = values.astype(jnp.bfloat16)
    lowered = lax.optimization_barrier(lowered)
    return lowered.astype(jnp.float32)

def reference(query_rows, key_rows, value_rows, forward_output, grad_output, log_normalizer, block_order, block_table):
    attn_scale = 1.0 / math.sqrt(DH)
    group_rows = 2 * BLK_ROWS
    row_index = jnp.arange(TOKENS, dtype=jnp.int32)
    seq_block = jnp.take(block_order, row_index // BLK_ROWS).astype(jnp.int32)
    position = (seq_block * BLK_ROWS + row_index % BLK_ROWS).astype(jnp.int32)
    key_groups = key_rows.astype(jnp.float32).reshape(N_BLK, group_rows, DH)
    value_groups = value_rows.astype(jnp.float32).reshape(N_BLK, group_rows, DH)
    query_groups = query_rows.astype(jnp.float32).reshape(N_BLK, group_rows, H, DH)
    grad_groups = grad_output.astype(jnp.float32).reshape(N_BLK, group_rows, H, DH)
    output_groups = forward_output.astype(jnp.float32).reshape(N_BLK, group_rows, H, DH)
    delta_groups = lax.optimization_barrier(jnp.sum(grad_groups * output_groups, axis=-1))
    norm_groups = log_normalizer.reshape(H, N_BLK, group_rows).transpose(1, 0, 2)
    pos_groups = position.reshape(N_BLK, group_rows)
    seq_groups = seq_block.reshape(N_BLK, group_rows)

    def one_group(sums, inputs):
        key_sum, value_sum = sums
        q_blk, g_blk, d_blk, l_blk, q_pos, q_seq, index = inputs
        grad_q = jnp.zeros((group_rows, H, DH), jnp.float32)
        table_rows = jnp.take(block_table, q_seq, axis=0)
        for turn in range(CYCLE_STEPS):
            owner = ((index - turn) % N_BLK).astype(jnp.int32)
            k_blk = key_groups[owner]
            v_blk = value_groups[owner]
            k_pos = pos_groups[owner]
            k_seq = seq_groups[owner]
            linked = jnp.take(table_rows, k_seq, axis=1) == 1
            allowed = (k_pos[None, :] <= q_pos[:, None]) & ((k_seq[None, :] == q_seq[:, None]) | linked)
            scores = jnp.einsum('qhd,kd->hqk', q_blk, k_blk, precision=lax.Precision.HIGHEST) * attn_scale
            probs = jnp.where(allowed[None], jnp.exp(scores - l_blk[:, :, None]), 0.0)
            probs_half = round_half(probs)
            value_part = jnp.einsum('hqk,qhd->kd', probs_half, g_blk, precision=lax.Precision.HIGHEST)
            grad_probs = jnp.einsum('qhd,kd->hqk', g_blk, v_blk, precision=lax.Precision.HIGHEST)
            grad_scores = round_half(probs * (grad_probs - d_blk.T[:, :, None]))
            grad_q = grad_q + jnp.einsum('hqk,kd->qhd', grad_scores, k_blk, precision=lax.Precision.HIGHEST) * attn_scale
            key_part = jnp.einsum('hqk,qhd->kd', grad_scores, q_blk, precision=lax.Precision.HIGHEST) * attn_scale
            key_sum = key_sum.at[owner].add(key_part)
            value_sum = value_sum.at[owner].add(value_part)
        return ((key_sum, value_sum), grad_q.astype(jnp.bfloat16))
    start_sums = (jnp.zeros((N_BLK, group_rows, DH), jnp.float32), jnp.zeros((N_BLK, group_rows, DH), jnp.float32))
    group_ids = jnp.arange(N_BLK, dtype=jnp.int32)
    final_sums, grad_q_groups = lax.scan(one_group, start_sums, (query_groups, grad_groups, delta_groups, norm_groups, pos_groups, seq_groups, group_ids))
    grad_query = grad_q_groups.reshape(TOKENS, H * DH)
    grad_key = final_sums[0].reshape(TOKENS, DH).astype(jnp.bfloat16)
    grad_value = final_sums[1].reshape(TOKENS, DH).astype(jnp.bfloat16)
    return (grad_query, grad_key, grad_value)
```

```python
import functools
import math

import jax
import jax.numpy as jnp
from jax import lax
from jax.experimental import pallas as pl
from jax.experimental.pallas import tpu as pltpu
from jax.sharding import PartitionSpec as P

BF16 = jnp.bfloat16
F32 = jnp.float32
BIG = 2.0**100
HEADS = 8
DH = 128
ROWS = 256
PIECE = 128
PARTS = 2
COLS = HEADS * PIECE
GROUPS = 32
SCALE = 1.0 / math.sqrt(DH)
EXP_SCALE = SCALE * math.log2(math.e)


def dot(a, b):
    return jnp.dot(a, b, preferred_element_type=F32)


def three_terms(column):
    high = column.astype(BF16)
    rest = column - high.astype(F32)
    middle = rest.astype(BF16)
    low = (rest - middle.astype(F32)).astype(BF16)
    return high.astype(F32), middle.astype(F32), low.astype(F32)


def extra_columns(column, lane):
    high, middle, low = three_terms(column)
    block = jnp.where(lane == 0, high, jnp.where(lane == 1, middle, jnp.where(lane == 2, low, 0.0)))
    return jnp.where(lane == 3, 1.0, block).astype(BF16)


def kernel(
    order_ref, table_ref, q_ref, k_ref, v_ref, o_ref, g_ref, norm_ref,
    dq_ref, dk_ref, dv_ref,
    o_all, norm_all, k_nat, v_nat, k_aug, v_aug, q_aug, g_aug, q_t, g_t, mask_add,
    dq_acc, acc, stage1, stage2, chip_in, recv1, recv2, zsend, zrecv,
    o_send, o_recv, n_send, n_recv, kv_send, kv_recv, c_send, c_recv,
    r1_send, r1_recv, r1_local, r2_send, r2_recv, r2_local, z_send, z_recv,
):
    b = lax.axis_index("blk")
    u = lax.axis_index("uly")
    core = lax.rem(b, 2)
    even = core == 0
    even_b = b - core
    mate = b + 1 - 2 * core
    after = lax.rem(b + 1, GROUPS)
    before = lax.rem(b + GROUPS - 1, GROUPS)
    ux = u // 2
    uy = lax.rem(u, 2)
    peers = []
    for dx, dy in ((0, 1), (1, 0), (3, 0), (1, 1), (3, 1), (2, 0), (2, 1)):
        peers.append(lax.rem(ux + dx, 4) * 2 + lax.rem(uy + dy, 2))

    barrier = pltpu.get_barrier_semaphore()

    def greet(blk, uly):
        pl.semaphore_signal(barrier, inc=1, device_id={"blk": blk, "uly": uly})

    for peer in peers:
        greet(b, peer)
        greet(mate, peer)
    greet(after, u)
    greet(before, u)

    own_half = u // 4
    q_seq = order_ref[2 * b + own_half]

    def blocked(k_seq):
        seen = jnp.logical_and(k_seq < q_seq, table_ref[q_seq, k_seq] == 1)
        return jnp.where(seen, 0.0, -BIG)

    other_add = blocked(order_ref[2 * b + 1 - own_half])
    before_add0 = blocked(order_ref[2 * before])
    before_add1 = blocked(order_ref[2 * before + 1])

    sub = lax.broadcasted_iota(jnp.int32, (DH, COLS), 0)
    half_of = lax.broadcasted_iota(jnp.int32, (DH, COLS), 1) // (COLS // 2)

    def build_keys(slot, part, key_part, value_part, add0, add1):
        for owner in range(HEADS):
            cols = slice(owner * PIECE, (owner + 1) * PIECE)
            k_aug[slot, part, 0:DH, cols] = key_part(owner).T
            v_aug[slot, part, 0:DH, cols] = value_part(owner).T
        minus = jnp.where(sub < 3, -1.0, 0.0)
        add = jnp.where(half_of == 0, add0, add1)
        k_aug[slot, part, DH : 2 * DH, :] = jnp.where(sub == 3, add, minus).astype(BF16)
        v_aug[slot, part, DH : 2 * DH, :] = minus.astype(BF16)

    own_add0 = jnp.where(own_half == 0, 0.0, other_add)
    own_add1 = jnp.where(own_half == 0, other_add, 0.0)
    for part in range(PARTS):
        k_nat[core, part] = k_ref[:, part]
        v_nat[core, part] = v_ref[:, part]
        build_keys(
            core, part, lambda o: k_ref[o, part], lambda o: v_ref[o, part], own_add0, own_add1
        )
        row = lax.broadcasted_iota(jnp.int32, (ROWS, COLS), 0) + u * ROWS
        col = lax.broadcasted_iota(jnp.int32, (ROWS, COLS), 1)
        key = (col // PIECE) * ROWS + part * PIECE + col % PIECE
        hidden = jnp.logical_and(key // 1024 == own_half, key > row)
        mask_add[part] = jnp.where(hidden, -BIG, 0.0)
    q_t[...] = q_ref[...].T
    g_t[...] = g_ref[...].T
    dq_acc[...] = jnp.zeros_like(dq_acc)
    acc[...] = jnp.zeros_like(acc)
    o_all[u] = o_ref[u]
    norm_all[u] = norm_ref[u]

    pl.semaphore_wait(barrier, 16)

    kv_copies = []
    for part in range(PARTS):
        for which, (src, dst) in enumerate(((k_ref, k_nat), (v_ref, v_nat))):
            copy = pltpu.make_async_remote_copy(
                src_ref=src.at[:, part],
                dst_ref=dst.at[core, part],
                send_sem=kv_send.at[part, which],
                recv_sem=kv_recv.at[part, which],
                device_id={"blk": after, "uly": u},
            )
            copy.start()
            kv_copies.append(copy)
    o_copies = []
    for j, peer in enumerate(peers):
        for src, dst, send, recv in (
            (norm_ref, norm_all, n_send, n_recv),
            (o_ref, o_all, o_send, o_recv),
        ):
            copy = pltpu.make_async_remote_copy(
                src_ref=src.at[peer],
                dst_ref=dst.at[u],
                send_sem=send.at[j],
                recv_sem=recv.at[u],
                device_id={"blk": b, "uly": peer},
            )
            copy.start()
            o_copies.append(copy)

    def wait_into(dst, sem):
        pltpu.make_async_copy(dst, dst, sem).wait()

    def arrive_keys(part):
        slot = 1 - core
        for which, dst in enumerate((k_nat, v_nat)):
            wait_into(dst.at[slot, part], kv_recv.at[part, which])
        build_keys(
            slot, part, lambda o: k_nat[slot, part, o], lambda o: v_nat[slot, part, o],
            before_add0, before_add1,
        )

    lane = lax.broadcasted_iota(jnp.int32, (ROWS, DH), 1)

    def prepare(head):
        @pl.when(head != u)
        def _():
            wait_into(norm_all.at[head], n_recv.at[head])
            wait_into(o_all.at[head], o_recv.at[head])

        cols = pl.ds(pl.multiple_of(head * DH, DH), DH)
        q_head = q_ref[:, cols]
        g_head = g_ref[:, cols]
        norm = jnp.broadcast_to(norm_all[head], (DH, ROWS)).T / SCALE
        delta = jnp.sum(g_head.astype(F32) * o_all[head].astype(F32), axis=1, keepdims=True)
        q_aug[head, :, 0:DH] = q_head
        q_aug[head, :, DH : 2 * DH] = extra_columns(norm, lane)
        g_aug[head, :, 0:DH] = g_head
        g_aug[head, :, DH : 2 * DH] = extra_columns(delta, lane)

    def tile(slot, part, head, masked):
        rows = pl.ds(pl.multiple_of(head * DH, DH), DH)
        scores = dot(q_aug[head], k_aug[slot, part])
        if masked:
            scores = scores + mask_add[part]
        probs = jnp.exp2(scores * EXP_SCALE)
        grad_probs = dot(g_aug[head], v_aug[slot, part])
        grad_scores = (probs * grad_probs).astype(BF16)
        keys = k_nat[slot, part].reshape(COLS, DH)
        dq_acc[head] += dot(grad_scores, keys)
        return dot(q_t[rows], grad_scores), dot(g_t[rows], probs.astype(BF16))

    def pair_of(j):
        return lax.rem(ux + j + (j // 2) * (1 - 2 * lax.rem(j, 2)), 4)

    def pair_tiles(slot, part, pair, masked):
        key0, value0 = tile(slot, part, 2 * pair, masked)
        key1, value1 = tile(slot, part, 2 * pair + 1, masked)
        key_sum = key0 + key1
        value_sum = value0 + value1
        for owner in range(HEADS):
            cols = slice(owner * PIECE, (owner + 1) * PIECE)
            acc[slot, part, owner, 0:DH] += key_sum[:, cols]
            acc[slot, part, owner, DH : 2 * DH] += value_sum[:, cols]

    @pl.when(core == 1)
    def _():
        for part in range(PARTS):
            arrive_keys(part)

    def first_phase(masked):
        def step(j, carry):
            pair = pair_of(j)
            prepare(2 * pair)
            prepare(2 * pair + 1)
            for part in range(PARTS):
                pair_tiles(0, part, pair, masked)
            return carry

        lax.fori_loop(0, 4, step, 0)

    @pl.when(even)
    def _():
        first_phase(True)

    @pl.when(core == 1)
    def _():
        first_phase(False)

    mine = 4 * core
    theirs = 4 - mine
    for t in range(4):
        for part in range(PARTS):
            stage1[theirs + t, part] = acc[0, part, theirs + t].astype(BF16)
    chip_copy = pltpu.make_async_remote_copy(
        src_ref=stage1.at[pl.ds(theirs, 4)],
        dst_ref=chip_in,
        send_sem=c_send,
        recv_sem=c_recv,
        device_id={"blk": mate, "uly": u},
    )
    chip_copy.start()

    @pl.when(even)
    def _():
        arrive_keys(0)

    def second_phase(part, first, last, masked):
        def step(j, carry):
            pair_tiles(1, part, pair_of(j), masked)
            return carry

        lax.fori_loop(first, last, step, 0)

    def second(part, first, last):
        @pl.when(even)
        def _():
            second_phase(part, first, last, False)

        @pl.when(core == 1)
        def _():
            second_phase(part, first, last, True)

    second(0, 0, 1)

    chip_copy.wait()

    def r1_copy(t):
        owner = mine + t
        return pltpu.make_async_remote_copy(
            src_ref=stage1.at[owner],
            dst_ref=recv1.at[u],
            send_sem=r1_send.at[t],
            recv_sem=r1_recv.at[u],
            device_id={"blk": even_b, "uly": owner},
        )

    def is_self(t):
        return jnp.logical_and(even, mine + t == u)

    for t in range(4):
        owner = mine + t
        for part in range(PARTS):
            total = acc[0, part, owner] + chip_in[t, part].astype(F32)
            stage1[owner, part] = total.astype(BF16)

        @pl.when(jnp.logical_not(is_self(t)))
        def _():
            r1_copy(t).start()

    second(0, 1, 4)

    r2_copies = []

    def send_second(part):
        for owner in range(HEADS):
            stage2[part, owner] = acc[1, part, owner].astype(BF16)
        for j, peer in enumerate(peers):
            copy = pltpu.make_async_remote_copy(
                src_ref=stage2.at[part, peer],
                dst_ref=recv2.at[part, u],
                send_sem=r2_send.at[part, j],
                recv_sem=r2_recv.at[part, u],
                device_id={"blk": b, "uly": peer},
            )
            copy.start()
            r2_copies.append(copy)

    send_second(0)

    @pl.when(even)
    def _():
        arrive_keys(1)

    second(1, 0, 4)
    send_second(1)

    for head in range(HEADS):
        dq_ref[:, head * DH : (head + 1) * DH] = (dq_acc[head] * SCALE).astype(BF16)

    def write(part, total):
        rows = slice(part * PIECE, (part + 1) * PIECE)
        dk_ref[rows, :] = (total[0:DH] * SCALE).T.astype(BF16)
        dv_ref[rows, :] = total[DH : 2 * DH].T.astype(BF16)

    @pl.when(even)
    def _():
        totals = [jnp.zeros((2 * DH, PIECE), F32) for _ in range(PARTS)]
        for sender in range(HEADS):
            local = jnp.logical_and(u == sender, u < 4)

            @pl.when(jnp.logical_not(local))
            def _():
                wait_into(recv1.at[sender], r1_recv.at[sender])

            @pl.when(local)
            def _():
                recv1[sender] = stage1[sender]

            for part in range(PARTS):
                totals[part] = totals[part] + recv1[sender, part].astype(F32)
        for part in range(PARTS):
            write(part, totals[part])

    for part in range(PARTS):
        total = acc[1, part, u]
        for peer in peers:
            wait_into(recv2.at[part, peer], r2_recv.at[part, peer])
            total = total + recv2[part, peer].astype(F32)

        def z_copy():
            return pltpu.make_async_remote_copy(
                src_ref=zsend.at[part],
                dst_ref=zrecv.at[part],
                send_sem=z_send.at[part],
                recv_sem=z_recv.at[part],
                device_id={"blk": before, "uly": u},
            )

        @pl.when(even)
        def _():
            zsend[part] = total.astype(BF16)
            z_copy().start()

        @pl.when(core == 1)
        def _():
            wait_into(zrecv.at[part], z_recv.at[part])
            write(part, total + zrecv[part].astype(F32))

    for copy in kv_copies + o_copies + r2_copies:
        copy.wait_send()
    for t in range(4):
        @pl.when(jnp.logical_not(is_self(t)))
        def _():
            r1_copy(t).wait_send()

    @pl.when(even)
    def _():
        for part in range(PARTS):
            wait_into(zsend.at[part], z_send.at[part])


def body(query_rows, key_rows, value_rows, forward_output, grad_output, log_normalizer, block_order, block_table):
    vmem = pl.BlockSpec(memory_space=pltpu.VMEM)
    smem = pl.BlockSpec(memory_space=pltpu.SMEM)
    dma = pltpu.SemaphoreType.DMA
    scratch = [
        pltpu.VMEM((HEADS, ROWS, DH), BF16),
        pltpu.VMEM((HEADS, 1, ROWS), F32),
        pltpu.VMEM((2, PARTS, HEADS, PIECE, DH), BF16),
        pltpu.VMEM((2, PARTS, HEADS, PIECE, DH), BF16),
        pltpu.VMEM((2, PARTS, 2 * DH, COLS), BF16),
        pltpu.VMEM((2, PARTS, 2 * DH, COLS), BF16),
        pltpu.VMEM((HEADS, ROWS, 2 * DH), BF16),
        pltpu.VMEM((HEADS, ROWS, 2 * DH), BF16),
        pltpu.VMEM((HEADS * DH, ROWS), BF16),
        pltpu.VMEM((HEADS * DH, ROWS), BF16),
        pltpu.VMEM((PARTS, ROWS, COLS), F32),
        pltpu.VMEM((HEADS, ROWS, DH), F32),
        pltpu.VMEM((2, PARTS, HEADS, 2 * DH, PIECE), F32),
        pltpu.VMEM((HEADS, PARTS, 2 * DH, PIECE), BF16),
        pltpu.VMEM((PARTS, HEADS, 2 * DH, PIECE), BF16),
        pltpu.VMEM((4, PARTS, 2 * DH, PIECE), BF16),
        pltpu.VMEM((HEADS, PARTS, 2 * DH, PIECE), BF16),
        pltpu.VMEM((PARTS, HEADS, 2 * DH, PIECE), BF16),
        pltpu.VMEM((PARTS, 2 * DH, PIECE), BF16),
        pltpu.VMEM((PARTS, 2 * DH, PIECE), BF16),
        dma((7,)), dma((HEADS,)),
        dma((7,)), dma((HEADS,)),
        dma((PARTS, 2)), dma((PARTS, 2)),
        dma, dma,
        dma((4,)), dma((HEADS,)), dma,
        dma((PARTS, 7)), dma((PARTS, HEADS)), dma,
        dma((PARTS,)), dma((PARTS,)),
    ]
    return pl.pallas_call(
        kernel,
        out_shape=(
            jax.ShapeDtypeStruct((ROWS, HEADS * DH), BF16),
            jax.ShapeDtypeStruct((ROWS, DH), BF16),
            jax.ShapeDtypeStruct((ROWS, DH), BF16),
        ),
        in_specs=[smem, smem] + [vmem] * 6,
        out_specs=(vmem, vmem, vmem),
        scratch_shapes=scratch,
        compiler_params=pltpu.CompilerParams(
            collective_id=0, has_side_effects=True, vmem_limit_bytes=56 << 20
        ),
        cost_estimate=pl.CostEstimate(
            flops=10 * ROWS * HEADS * 4096 * DH,
            bytes_accessed=5 << 20,
            transcendentals=ROWS * HEADS * 4096,
        ),
    )(
        block_order,
        block_table,
        query_rows,
        key_rows.reshape(HEADS, PARTS, PIECE, DH),
        value_rows.reshape(HEADS, PARTS, PIECE, DH),
        forward_output.reshape(HEADS, ROWS, DH),
        grad_output,
        log_normalizer.reshape(HEADS, 1, ROWS),
    )


def solution(mesh):
    in_specs = (
        P(("blk", "uly"), None),
        P("blk", None),
        P("blk", None),
        P("blk", "uly"),
        P(("blk", "uly"), None),
        P("uly", "blk"),
        P(),
        P(),
    )
    out_specs = (P(("blk", "uly"), None), P(("blk", "uly"), None), P(("blk", "uly"), None))
    return jax.shard_map(body, mesh=mesh, in_specs=in_specs, out_specs=out_specs, check_vma=False)
```

```python
import functools
import math

import jax
import jax.numpy as jnp
from jax import lax
from jax.experimental import pallas as pl
from jax.experimental.pallas import tpu as pltpu
from jax.sharding import PartitionSpec as P

BF16 = jnp.bfloat16
F32 = jnp.float32
BIG = 2.0**100
HEADS = 8
DH = 128
ROWS = 256
PIECE = 128
PARTS = 2
COLS = HEADS * PIECE
GROUPS = 32
PLANE = 16
SCALE = 1.0 / math.sqrt(DH)
EXP_SCALE = SCALE * math.log2(math.e)


def dot(a, b):
    return jnp.dot(a, b, preferred_element_type=F32)


def three_terms(column):
    high = column.astype(BF16)
    rest = column - high.astype(F32)
    middle = rest.astype(BF16)
    low = (rest - middle.astype(F32)).astype(BF16)
    return high.astype(F32), middle.astype(F32), low.astype(F32)


def extra_columns(column, lane):
    high, middle, low = three_terms(column)
    block = jnp.where(lane == 0, high, jnp.where(lane == 1, middle, jnp.where(lane == 2, low, 0.0)))
    return jnp.where(lane == 3, 1.0, block).astype(BF16)


def kernel(
    order_ref, table_ref, q_ref, k_ref, v_ref, o_ref, g_ref, norm_ref,
    dq_ref, dkv_ref,
    o_all, norm_all, kv_nat, k_aug, v_aug, q_aug, g_aug, q_t, g_t, mask_add,
    dq_acc, acc, probs_kept, stage1, stage2, chip_in, recv1, recv2, zsend, zrecv, sums,
    o_send, o_recv, n_send, n_recv, kv_send, kv_recv, w_send, w_recv, f_send, f_recv,
    c_send, c_recv, r1_send, r1_recv, r2_send, r2_recv, z_send, z_recv,
):
    b = lax.axis_index("blk")
    u = lax.axis_index("uly")
    core = lax.rem(b, 2)
    even = core == 0
    odd = core == 1
    even_b = b - core
    mate = b + 1 - 2 * core
    after = lax.rem(b + 1, GROUPS)
    before = lax.rem(b + GROUPS - 1, GROUPS)
    far_sender = lax.rem(b, PLANE) == PLANE - 1
    far_receiver = lax.rem(b, PLANE) == 0
    ux = u // 2
    uy = lax.rem(u, 2)
    peers = []
    for dx, dy in ((0, 1), (1, 0), (3, 0), (1, 1), (3, 1), (2, 0), (2, 1)):
        peers.append(lax.rem(ux + dx, 4) * 2 + lax.rem(uy + dy, 2))

    barrier = pltpu.get_barrier_semaphore()

    def greet(blk, uly):
        pl.semaphore_signal(barrier, inc=1, device_id={"blk": blk, "uly": uly})

    greet(mate, u)
    for peer in peers:
        greet(b, peer)
        greet(mate, peer)

    @pl.when(even)
    def _():
        greet(before, u)

    for part in range(PARTS):
        kv_nat[core, part, 0] = k_ref[:, part]
        kv_nat[core, part, 1] = v_ref[:, part]
    o_all[u] = o_ref[u]
    norm_all[u] = norm_ref[u]

    @pl.when(even)
    def _():
        pl.semaphore_wait(barrier, 15)

    @pl.when(odd)
    def _():
        pl.semaphore_wait(barrier, 16)

    def o_copies(j):
        peer = peers[j]
        copies = []
        for src, dst, send, recv in (
            (norm_ref, norm_all, n_send, n_recv),
            (o_ref, o_all, o_send, o_recv),
        ):
            copies.append(pltpu.make_async_remote_copy(
                src_ref=src.at[peer],
                dst_ref=dst.at[u],
                send_sem=send.at[j],
                recv_sem=recv.at[u],
                device_id={"blk": b, "uly": peer},
            ))
        return copies

    def kv_copy(part):
        return pltpu.make_async_remote_copy(
            src_ref=kv_nat.at[core, part],
            dst_ref=kv_nat.at[core, part],
            send_sem=kv_send.at[part],
            recv_sem=kv_recv.at[part],
            device_id={"blk": after, "uly": u},
        )

    def quarter(slot, half, x):
        return kv_nat.at[slot, half, :, pl.ds(2 * x, 2)]

    def far_copy(half):
        return pltpu.make_async_remote_copy(
            src_ref=quarter(core, half, ux),
            dst_ref=quarter(core, half, ux),
            send_sem=w_send.at[half],
            recv_sem=w_recv.at[half],
            device_id={"blk": after, "uly": u},
        )

    def forward_copy(half, dx):
        return pltpu.make_async_remote_copy(
            src_ref=quarter(1 - core, half, ux),
            dst_ref=quarter(1 - core, half, ux),
            send_sem=f_send.at[half, dx],
            recv_sem=f_recv.at[half, ux],
            device_id={"blk": b, "uly": lax.rem(ux + dx, 4) * 2 + uy},
        )

    @pl.when(far_sender)
    def _():
        for half in range(2):
            far_copy(half).start()

    @pl.when(jnp.logical_not(far_sender))
    def _():
        for part in range(PARTS):
            kv_copy(part).start()

    for j in range(7):
        for copy in o_copies(j):
            copy.start()

    own_half = u // 4
    q_seq = order_ref[2 * b + own_half]

    def blocked(k_seq):
        seen = jnp.logical_and(k_seq < q_seq, table_ref[q_seq, k_seq] == 1)
        return jnp.where(seen, 0.0, -BIG)

    other_add = blocked(order_ref[2 * b + 1 - own_half])
    before_add0 = blocked(order_ref[2 * before])
    before_add1 = blocked(order_ref[2 * before + 1])
    own_add0 = jnp.where(own_half == 0, 0.0, other_add)
    own_add1 = jnp.where(own_half == 0, other_add, 0.0)

    def build_keys(slot, part, add0, add1):
        sub = lax.broadcasted_iota(jnp.int32, (DH, COLS), 0)
        half_of = lax.broadcasted_iota(jnp.int32, (DH, COLS), 1) // (COLS // 2)
        k_aug[slot, part, 0:DH, :] = kv_nat[slot, part, 0].reshape(COLS, DH).T
        v_aug[slot, part, 0:DH, :] = kv_nat[slot, part, 1].reshape(COLS, DH).T
        minus = jnp.where(sub < 3, -1.0, 0.0)
        add = jnp.where(half_of == 0, add0, add1)
        k_aug[slot, part, DH : 2 * DH, :] = jnp.where(sub == 3, add, minus).astype(BF16)
        v_aug[slot, part, DH : 2 * DH, :] = minus.astype(BF16)

    def own_part(part, carry):
        build_keys(core, part, own_add0, own_add1)
        row = lax.broadcasted_iota(jnp.int32, (ROWS, COLS), 0) + u * ROWS
        col = lax.broadcasted_iota(jnp.int32, (ROWS, COLS), 1)
        key = (col // PIECE) * ROWS + part * PIECE + col % PIECE
        hidden = jnp.logical_and(col // (COLS // 2) == own_half, key > row)
        mask_add[part] = jnp.where(hidden, -BIG, 0.0)
        for which in range(2):
            acc[part, which] = jnp.zeros((DH, COLS), F32)
        return carry

    lax.fori_loop(0, PARTS, own_part, 0)
    for src, dst in ((q_ref, q_t), (g_ref, g_t)):
        turned = src[...].T
        for head in range(HEADS):
            cols = slice(head % 2 * ROWS, (head % 2 + 1) * ROWS)
            dst[head // 2, :, cols] = turned[head * DH : (head + 1) * DH]
    dq_acc[...] = jnp.zeros_like(dq_acc)

    def wait_into(dst, sem):
        pltpu.make_async_copy(dst, dst, sem).wait()

    def arrive_keys(half):
        slot = 1 - core

        @pl.when(far_receiver)
        def _():
            for dx in (1, 3, 2):
                x = lax.rem(ux + dx, 4)
                wait_into(quarter(slot, half, x), f_recv.at[half, x])

        @pl.when(jnp.logical_not(far_receiver))
        def _():
            wait_into(kv_nat.at[slot, half], kv_recv.at[half])

        build_keys(slot, half, before_add0, before_add1)

    lane = lax.broadcasted_iota(jnp.int32, (ROWS, DH), 1)

    def prepare(pair, member):
        head = 2 * pair + member

        @pl.when(head != u)
        def _():
            wait_into(norm_all.at[head], n_recv.at[head])
            wait_into(o_all.at[head], o_recv.at[head])

        cols = pl.ds(pl.multiple_of(head * DH, DH), DH)
        rows = slice(member * ROWS, (member + 1) * ROWS)
        q_head = q_ref[:, cols]
        g_head = g_ref[:, cols]
        norm = jnp.broadcast_to(norm_all[head], (DH, ROWS)).T / SCALE
        delta = jnp.sum(g_head.astype(F32) * o_all[head].astype(F32), axis=1, keepdims=True)
        q_aug[pair, rows, 0:DH] = q_head
        q_aug[pair, rows, DH : 2 * DH] = extra_columns(norm, lane)
        g_aug[pair, rows, 0:DH] = g_head
        g_aug[pair, rows, DH : 2 * DH] = extra_columns(delta, lane)

    def tile_probs(slot, part, pair, masked):
        scores = dot(q_aug[pair], k_aug[slot, part])
        if masked:
            scores = scores.reshape(2, ROWS, COLS) + mask_add[part][None]
            scores = scores.reshape(2 * ROWS, COLS)
        return jnp.exp2(scores * EXP_SCALE)

    def tile_keys(slot, part, pair, probs):
        grad_probs = dot(g_aug[pair], v_aug[slot, part])
        grad_scores = (probs * grad_probs).astype(BF16)
        dq_acc[pair] += dot(grad_scores, kv_nat[slot, part, 0].reshape(COLS, DH))
        return dot(q_t[pair], grad_scores)

    def tile_values(pair, probs):
        return dot(g_t[pair], probs.astype(BF16))

    def put_pieces(stage, total):
        for owner in range(HEADS):
            stage[owner] = total[:, owner * PIECE : (owner + 1) * PIECE].astype(BF16)

    def first_pairs(half, first, last, masked):
        def step(j, carry):
            pair = lax.rem(ux + j + (j // 2) * (1 - 2 * lax.rem(j, 2)), 4)
            if half == 0:
                prepare(pair, 0)
                prepare(pair, 1)
            probs = tile_probs(0, half, pair, masked)
            acc[half, 0] += tile_keys(0, half, pair, probs)
            acc[half, 1] += tile_values(pair, probs)
            return carry

        lax.fori_loop(first, last, step, 0)

    def first(half, first_pair, last_pair):
        @pl.when(even)
        def _():
            first_pairs(half, first_pair, last_pair, True)

        @pl.when(odd)
        def _():
            first_pairs(half, first_pair, last_pair, False)

    mine = 4 * core
    theirs = 4 - mine

    def chip_copy(half):
        return pltpu.make_async_remote_copy(
            src_ref=stage1.at[half, :, pl.ds(theirs, 4)],
            dst_ref=chip_in.at[half],
            send_sem=c_send.at[half],
            recv_sem=c_recv.at[half],
            device_id={"blk": mate, "uly": u},
        )

    def exchange(half):
        for which in range(2):
            put_pieces(stage1.at[half, which], acc[half, which])
        chip_copy(half).start()

    def r1_copy(half, t):
        owner = mine + t
        return pltpu.make_async_remote_copy(
            src_ref=stage1.at[half, :, owner],
            dst_ref=recv1.at[half, u],
            send_sem=r1_send.at[half, t],
            recv_sem=r1_recv.at[half, u],
            device_id={"blk": even_b, "uly": owner},
        )

    def is_self(t):
        return jnp.logical_and(even, mine + t == u)

    def combine(half):
        wait_into(chip_in.at[half], c_recv.at[half])
        for t in range(4):
            for which in range(2):
                total = stage1[half, which, mine + t].astype(F32) + chip_in[half, which, t].astype(F32)
                stage1[half, which, mine + t] = total.astype(BF16)

            @pl.when(jnp.logical_not(is_self(t)))
            def _():
                r1_copy(half, t).start()

    def r2_copy(part, which, j):
        peer = peers[j]
        return pltpu.make_async_remote_copy(
            src_ref=stage2.at[part, which, peer],
            dst_ref=recv2.at[part, which, u],
            send_sem=r2_send.at[part, which, j],
            recv_sem=r2_recv.at[part, which, u],
            device_id={"blk": b, "uly": peer},
        )

    def second_values(part, masked):
        total = None
        for pair in range(HEADS // 2):
            probs = tile_probs(1, part, pair, masked)
            probs_kept[pair] = probs
            term = tile_values(pair, probs)
            total = term if total is None else total + term
        put_pieces(stage2.at[part, 1], total)

    def second_keys(part):
        total = None
        for pair in range(HEADS // 2):
            term = tile_keys(1, part, pair, probs_kept[pair])
            total = term if total is None else total + term
        put_pieces(stage2.at[part, 0], total)

    @pl.when(odd)
    def _():
        arrive_keys(0)
        arrive_keys(1)

    first(0, 0, 4)
    exchange(0)
    first(1, 0, 1)
    combine(0)

    @pl.when(far_receiver)
    def _():
        for half in range(2):
            wait_into(quarter(1 - core, half, ux), w_recv.at[half])
            for dx in (1, 3, 2):
                forward_copy(half, dx).start()

    first(1, 1, 4)
    exchange(1)

    @pl.when(even)
    def _():
        arrive_keys(0)

    def second_step(part, carry):
        @pl.when(jnp.logical_and(even, part == 1))
        def _():
            arrive_keys(1)

        @pl.when(even)
        def _():
            second_values(part, False)

        @pl.when(odd)
        def _():
            second_values(part, True)

        @pl.when(part == 0)
        def _():
            combine(1)

        for j in range(7):
            r2_copy(part, 1, j).start()
        second_keys(part)
        for j in range(7):
            r2_copy(part, 0, j).start()
        return carry

    lax.fori_loop(0, PARTS, second_step, 0)

    for head in range(HEADS):
        rows = slice(head % 2 * ROWS, (head % 2 + 1) * ROWS)
        dq_ref[:, head * DH : (head + 1) * DH] = (dq_acc[head // 2, rows] * SCALE).astype(BF16)

    def write(part, which, total):
        rows = slice(part * PIECE, (part + 1) * PIECE)
        turned = total.T
        if which == 0:
            turned = turned * SCALE
        dkv_ref[which, rows, :] = turned.astype(BF16)

    @pl.when(even)
    def _():
        for half in range(2):
            for sender in range(HEADS):
                local = jnp.logical_and(u == sender, u < 4)

                @pl.when(jnp.logical_not(local))
                def _():
                    wait_into(recv1.at[half, sender], r1_recv.at[half, sender])

                @pl.when(local)
                def _():
                    for which in range(2):
                        recv1[half, sender, which] = stage1[half, which, sender]

            for which in range(2):
                total = recv1[half, 0, which].astype(F32)
                for sender in range(1, HEADS):
                    total = total + recv1[half, sender, which].astype(F32)
                write(half, which, total)

    def z_copy(part, which):
        return pltpu.make_async_remote_copy(
            src_ref=zsend.at[part, which],
            dst_ref=zrecv.at[part, which],
            send_sem=z_send.at[part, which],
            recv_sem=z_recv.at[part, which],
            device_id={"blk": before, "uly": u},
        )

    steps = [(part, which) for part in range(PARTS) for which in (1, 0)]
    for part, which in steps:
        total = stage2[part, which, u].astype(F32)
        for peer in peers:
            wait_into(recv2.at[part, which, peer], r2_recv.at[part, which, peer])
            total = total + recv2[part, which, peer].astype(F32)

        @pl.when(even)
        def _():
            zsend[part, which] = total.astype(BF16)
            z_copy(part, which).start()

        @pl.when(odd)
        def _():
            sums[part, which] = total

    @pl.when(odd)
    def _():
        for part, which in steps:
            wait_into(zrecv.at[part, which], z_recv.at[part, which])
            write(part, which, sums[part, which] + zrecv[part, which].astype(F32))

    for j in range(7):
        for copy in o_copies(j):
            copy.wait_send()

    @pl.when(far_sender)
    def _():
        for half in range(2):
            far_copy(half).wait_send()

    @pl.when(jnp.logical_not(far_sender))
    def _():
        for part in range(PARTS):
            kv_copy(part).wait_send()

    @pl.when(far_receiver)
    def _():
        for half in range(2):
            for dx in (1, 3, 2):
                forward_copy(half, dx).wait_send()

    for half in range(2):
        chip_copy(half).wait_send()
        for t in range(4):
            @pl.when(jnp.logical_not(is_self(t)))
            def _():
                r1_copy(half, t).wait_send()

    for part, which in steps:
        for j in range(7):
            r2_copy(part, which, j).wait_send()

        @pl.when(even)
        def _():
            z_copy(part, which).wait_send()


def hand_on(dq_in, dkv_in, dq_ref, dk_ref, dv_ref):
    dq_ref[...] = dq_in[...]
    dk_ref[...] = dkv_in[0]
    dv_ref[...] = dkv_in[1]


def body(query_rows, key_rows, value_rows, forward_output, grad_output, log_normalizer, block_order, block_table):
    vmem = pl.BlockSpec(memory_space=pltpu.VMEM)
    smem = pl.BlockSpec(memory_space=pltpu.SMEM)
    dma = pltpu.SemaphoreType.DMA
    piece = (DH, PIECE)
    scratch = [
        pltpu.VMEM((HEADS, ROWS, DH), BF16),
        pltpu.VMEM((HEADS, 1, ROWS), F32),
        pltpu.VMEM((2, PARTS, 2, HEADS, PIECE, DH), BF16),
        pltpu.VMEM((2, PARTS, 2 * DH, COLS), BF16),
        pltpu.VMEM((2, PARTS, 2 * DH, COLS), BF16),
        pltpu.VMEM((HEADS // 2, 2 * ROWS, 2 * DH), BF16),
        pltpu.VMEM((HEADS // 2, 2 * ROWS, 2 * DH), BF16),
        pltpu.VMEM((HEADS // 2, DH, 2 * ROWS), BF16),
        pltpu.VMEM((HEADS // 2, DH, 2 * ROWS), BF16),
        pltpu.VMEM((PARTS, ROWS, COLS), F32),
        pltpu.VMEM((HEADS // 2, 2 * ROWS, DH), F32),
        pltpu.VMEM((PARTS, 2, DH, COLS), F32),
        pltpu.VMEM((HEADS // 2, 2 * ROWS, COLS), F32),
        pltpu.VMEM((PARTS, 2, HEADS) + piece, BF16),
        pltpu.VMEM((PARTS, 2, HEADS) + piece, BF16),
        pltpu.VMEM((PARTS, 2, 4) + piece, BF16),
        pltpu.VMEM((PARTS, HEADS, 2) + piece, BF16),
        pltpu.VMEM((PARTS, 2, HEADS) + piece, BF16),
        pltpu.VMEM((PARTS, 2) + piece, BF16),
        pltpu.VMEM((PARTS, 2) + piece, BF16),
        pltpu.VMEM((PARTS, 2) + piece, F32),
        dma((7,)), dma((HEADS,)),
        dma((7,)), dma((HEADS,)),
        dma((PARTS,)), dma((PARTS,)),
        dma((2,)), dma((2,)),
        dma((2, 4)), dma((2, 4)),
        dma((2,)), dma((2,)),
        dma((2, 4)), dma((2, HEADS)),
        dma((PARTS, 2, 7)), dma((PARTS, 2, HEADS)),
        dma((PARTS, 2)), dma((PARTS, 2)),
    ]
    dq, dkv = pl.pallas_call(
        kernel,
        out_shape=(
            jax.ShapeDtypeStruct((ROWS, HEADS * DH), BF16),
            jax.ShapeDtypeStruct((2, ROWS, DH), BF16),
        ),
        in_specs=[smem, smem] + [vmem] * 6,
        out_specs=(vmem, vmem),
        scratch_shapes=scratch,
        compiler_params=pltpu.CompilerParams(
            collective_id=0, has_side_effects=True, vmem_limit_bytes=56 << 20
        ),
        cost_estimate=pl.CostEstimate(
            flops=10 * ROWS * HEADS * 4096 * DH,
            bytes_accessed=5 << 20,
            transcendentals=ROWS * HEADS * 4096,
        ),
    )(
        block_order,
        block_table,
        query_rows,
        key_rows.reshape(HEADS, PARTS, PIECE, DH),
        value_rows.reshape(HEADS, PARTS, PIECE, DH),
        forward_output.reshape(HEADS, ROWS, DH),
        grad_output,
        log_normalizer.reshape(HEADS, 1, ROWS),
    )
    rows_out = jax.ShapeDtypeStruct((ROWS, DH), BF16)
    return pl.pallas_call(
        hand_on,
        out_shape=(jax.ShapeDtypeStruct((ROWS, HEADS * DH), BF16), rows_out, rows_out),
        in_specs=[vmem, vmem],
        out_specs=(vmem, vmem, vmem),
    )(dq, dkv)


def solution(mesh):
    in_specs = (
        P(("blk", "uly"), None),
        P("blk", None),
        P("blk", None),
        P("blk", "uly"),
        P(("blk", "uly"), None),
        P("uly", "blk"),
        P(),
        P(),
    )
    out_specs = (P(("blk", "uly"), None), P(("blk", "uly"), None), P(("blk", "uly"), None))
    return jax.shard_map(body, mesh=mesh, in_specs=in_specs, out_specs=out_specs, check_vma=False)
```

```python
import functools
import math

import jax
import jax.numpy as jnp
from jax import lax
from jax.experimental import pallas as pl
from jax.experimental.pallas import tpu as pltpu
from jax.sharding import PartitionSpec as P

BF16 = jnp.bfloat16
F32 = jnp.float32
BIG = 2.0**100
HEADS = 8
DH = 128
ROWS = 256
PIECE = 128
PARTS = 2
COLS = HEADS * PIECE
GROUPS = 32
PLANE = 16
SCALE = 1.0 / math.sqrt(DH)
EXP_SCALE = SCALE * math.log2(math.e)


def dot(a, b):
    return jnp.dot(a, b, preferred_element_type=F32)


def three_terms(column):
    high = column.astype(BF16)
    rest = column - high.astype(F32)
    middle = rest.astype(BF16)
    low = (rest - middle.astype(F32)).astype(BF16)
    return high.astype(F32), middle.astype(F32), low.astype(F32)


def extra_columns(column, lane):
    high, middle, low = three_terms(column)
    block = jnp.where(lane == 0, high, jnp.where(lane == 1, middle, jnp.where(lane == 2, low, 0.0)))
    return jnp.where(lane == 3, 1.0, block).astype(BF16)


def kernel(
    order_ref, table_ref, q_ref, k_ref, v_ref, o_ref, g_ref, norm_ref,
    dq_ref, dkv_ref,
    o_all, norm_all, kv_nat, k_aug, v_aug, q_aug, g_aug, q_t, g_t, mask_add,
    dq_acc, acc, probs_kept, stage, chip_in, recv1, recv2, zsend, zrecv, sums,
    o_send, o_recv, n_send, n_recv, kv_send, kv_recv, w_send, w_recv, f_send, f_recv,
    c_send, c_recv, r1_send, r1_recv, r2_send, r2_recv, z_send, z_recv,
):
    b = lax.axis_index("blk")
    u = lax.axis_index("uly")
    core = lax.rem(b, 2)
    even = core == 0
    odd = core == 1
    even_b = b - core
    mate = b + 1 - 2 * core
    after = lax.rem(b + 1, GROUPS)
    before = lax.rem(b + GROUPS - 1, GROUPS)
    far_sender = lax.rem(b, PLANE) == PLANE - 1
    far_receiver = lax.rem(b, PLANE) == 0
    ux = u // 2
    uy = lax.rem(u, 2)
    peers = []
    for dx, dy in ((0, 1), (1, 0), (3, 0), (1, 1), (3, 1), (2, 0), (2, 1)):
        peers.append(lax.rem(ux + dx, 4) * 2 + lax.rem(uy + dy, 2))

    barrier = pltpu.get_barrier_semaphore()

    def greet(blk, uly):
        pl.semaphore_signal(barrier, inc=1, device_id={"blk": blk, "uly": uly})

    greet(mate, u)
    for peer in peers:
        greet(b, peer)
        greet(mate, peer)

    @pl.when(even)
    def _():
        greet(before, u)

    for part in range(PARTS):
        kv_nat[core, part, 0] = k_ref[:, part]
        kv_nat[core, part, 1] = v_ref[:, part]
    o_all[u] = o_ref[u]
    norm_all[u] = norm_ref[u]

    @pl.when(even)
    def _():
        pl.semaphore_wait(barrier, 15)

    @pl.when(odd)
    def _():
        pl.semaphore_wait(barrier, 16)

    def norm_copy(j):
        return pltpu.make_async_remote_copy(
            src_ref=norm_ref.at[peers[j]],
            dst_ref=norm_all.at[u],
            send_sem=n_send.at[j],
            recv_sem=n_recv.at[u],
            device_id={"blk": b, "uly": peers[j]},
        )

    def o_copy(j):
        return pltpu.make_async_remote_copy(
            src_ref=o_ref.at[peers[j]],
            dst_ref=o_all.at[u],
            send_sem=o_send.at[j],
            recv_sem=o_recv.at[u],
            device_id={"blk": b, "uly": peers[j]},
        )

    def kv_copy(part):
        return pltpu.make_async_remote_copy(
            src_ref=kv_nat.at[core, part],
            dst_ref=kv_nat.at[core, part],
            send_sem=kv_send.at[part],
            recv_sem=kv_recv.at[part],
            device_id={"blk": after, "uly": u},
        )

    def quarter(slot, half, x):
        return kv_nat.at[slot, half, :, pl.ds(2 * x, 2)]

    def far_copy(half):
        return pltpu.make_async_remote_copy(
            src_ref=quarter(core, half, ux),
            dst_ref=quarter(core, half, ux),
            send_sem=w_send.at[half],
            recv_sem=w_recv.at[half],
            device_id={"blk": after, "uly": u},
        )

    def forward_copy(half, dx):
        return pltpu.make_async_remote_copy(
            src_ref=quarter(1 - core, half, ux),
            dst_ref=quarter(1 - core, half, ux),
            send_sem=f_send.at[half, dx],
            recv_sem=f_recv.at[half, ux],
            device_id={"blk": b, "uly": lax.rem(ux + dx, 4) * 2 + uy},
        )

    for j in range(7):
        norm_copy(j).start()

    @pl.when(far_sender)
    def _():
        for half in range(2):
            far_copy(half).start()

    @pl.when(jnp.logical_not(far_sender))
    def _():
        for part in range(PARTS):
            kv_copy(part).start()

    for j in range(7):
        o_copy(j).start()

    own_half = u // 4
    q_seq = order_ref[2 * b + own_half]

    def blocked(k_seq):
        seen = jnp.logical_and(k_seq < q_seq, table_ref[q_seq, k_seq] == 1)
        return jnp.where(seen, 0.0, -BIG)

    other_add = blocked(order_ref[2 * b + 1 - own_half])
    before_add0 = blocked(order_ref[2 * before])
    before_add1 = blocked(order_ref[2 * before + 1])
    own_add0 = jnp.where(own_half == 0, 0.0, other_add)
    own_add1 = jnp.where(own_half == 0, other_add, 0.0)

    def build_keys(slot, part, add0, add1):
        sub = lax.broadcasted_iota(jnp.int32, (DH, COLS), 0)
        half_of = lax.broadcasted_iota(jnp.int32, (DH, COLS), 1) // (COLS // 2)
        k_aug[slot, part, 0:DH, :] = kv_nat[slot, part, 0].reshape(COLS, DH).T
        v_aug[slot, part, 0:DH, :] = kv_nat[slot, part, 1].reshape(COLS, DH).T
        minus = jnp.where(sub < 3, -1.0, 0.0)
        add = jnp.where(half_of == 0, add0, add1)
        k_aug[slot, part, DH : 2 * DH, :] = jnp.where(sub == 3, add, minus).astype(BF16)
        v_aug[slot, part, DH : 2 * DH, :] = minus.astype(BF16)

    def own_part(part, carry):
        build_keys(core, part, own_add0, own_add1)
        row = lax.broadcasted_iota(jnp.int32, (ROWS, COLS), 0) + u * ROWS
        col = lax.broadcasted_iota(jnp.int32, (ROWS, COLS), 1)
        key = (col // PIECE) * ROWS + part * PIECE + col % PIECE
        hidden = jnp.logical_and(col // (COLS // 2) == own_half, key > row)
        mask_add[part] = jnp.where(hidden, -BIG, 0.0)
        return carry

    lax.fori_loop(0, PARTS, own_part, 0)
    for src, dst in ((q_ref, q_t), (g_ref, g_t)):
        turned = src[...].T
        for head in range(HEADS):
            cols = slice(head % 2 * ROWS, (head % 2 + 1) * ROWS)
            dst[head // 2, :, cols] = turned[head * DH : (head + 1) * DH]
    dq_acc[...] = jnp.zeros_like(dq_acc)

    def wait_into(dst, sem):
        pltpu.make_async_copy(dst, dst, sem).wait()

    def arrive_keys(half):
        slot = 1 - core

        @pl.when(far_receiver)
        def _():
            for dx in (1, 3, 2):
                x = lax.rem(ux + dx, 4)
                wait_into(quarter(slot, half, x), f_recv.at[half, x])

        @pl.when(jnp.logical_not(far_receiver))
        def _():
            wait_into(kv_nat.at[slot, half], kv_recv.at[half])

        build_keys(slot, half, before_add0, before_add1)

    lane = lax.broadcasted_iota(jnp.int32, (ROWS, DH), 1)

    def prepare_queries(pair, member):
        head = 2 * pair + member

        @pl.when(head != u)
        def _():
            wait_into(norm_all.at[head], n_recv.at[head])

        cols = pl.ds(pl.multiple_of(head * DH, DH), DH)
        rows = slice(member * ROWS, (member + 1) * ROWS)
        norm = jnp.broadcast_to(norm_all[head], (DH, ROWS)).T / SCALE
        q_aug[pair, rows, 0:DH] = q_ref[:, cols]
        q_aug[pair, rows, DH : 2 * DH] = extra_columns(norm, lane)

    def prepare_grads(pair, member):
        head = 2 * pair + member

        @pl.when(head != u)
        def _():
            wait_into(o_all.at[head], o_recv.at[head])

        cols = pl.ds(pl.multiple_of(head * DH, DH), DH)
        rows = slice(member * ROWS, (member + 1) * ROWS)
        g_head = g_ref[:, cols]
        delta = jnp.sum(g_head.astype(F32) * o_all[head].astype(F32), axis=1, keepdims=True)
        g_aug[pair, rows, 0:DH] = g_head
        g_aug[pair, rows, DH : 2 * DH] = extra_columns(delta, lane)

    def tile_probs(slot, part, pair, masked):
        scores = dot(q_aug[pair], k_aug[slot, part])
        if masked:
            scores = scores.reshape(2, ROWS, COLS) + mask_add[part][None]
            scores = scores.reshape(2 * ROWS, COLS)
        return jnp.exp2(scores * EXP_SCALE)

    def tile_keys(slot, part, pair, probs):
        grad_probs = dot(g_aug[pair], v_aug[slot, part])
        grad_scores = (probs * grad_probs).astype(BF16)
        dq_acc[pair] += dot(grad_scores, kv_nat[slot, part, 0].reshape(COLS, DH))
        return dot(q_t[pair], grad_scores)

    def tile_values(pair, probs):
        return dot(g_t[pair], probs.astype(BF16))

    def put_pieces(stage, total):
        for owner in range(HEADS):
            stage[owner] = total[:, owner * PIECE : (owner + 1) * PIECE].astype(BF16)

    def pair_of(j):
        return lax.rem(ux + j + (j // 2) * (1 - 2 * lax.rem(j, 2)), 4)

    def value_sums(step, slot, part, masked):
        def two(i, carry):
            pairs = (pair_of(2 * i), pair_of(2 * i + 1))

            @pl.when(step == 0)
            def _():
                for pair in pairs:
                    prepare_queries(pair, 0)
                    prepare_queries(pair, 1)

            total = None
            for pair in pairs:
                probs = tile_probs(slot, part, pair, masked)
                probs_kept[pair] = probs
                term = tile_values(pair, probs)
                total = term if total is None else total + term
            acc[1] += total
            return carry

        lax.fori_loop(0, 2, two, 0)

    def key_sums(step, slot, part):
        def two(i, carry):
            pairs = (pair_of(2 * i), pair_of(2 * i + 1))

            @pl.when(step == 0)
            def _():
                for pair in pairs:
                    prepare_grads(pair, 0)
                    prepare_grads(pair, 1)

            total = None
            for pair in pairs:
                term = tile_keys(slot, part, pair, probs_kept[pair])
                total = term if total is None else total + term
            acc[0] += total
            return carry

        lax.fori_loop(0, 2, two, 0)

    mine = 4 * core
    theirs = 4 - mine

    def chip_copy(half, which):
        return pltpu.make_async_remote_copy(
            src_ref=stage.at[0, half, which, pl.ds(theirs, 4)],
            dst_ref=chip_in.at[half, which],
            send_sem=c_send.at[half, which],
            recv_sem=c_recv.at[half, which],
            device_id={"blk": mate, "uly": u},
        )

    def r1_copy(half, which, t):
        owner = mine + t
        return pltpu.make_async_remote_copy(
            src_ref=stage.at[0, half, which, owner],
            dst_ref=recv1.at[half, which, u],
            send_sem=r1_send.at[half, which, t],
            recv_sem=r1_recv.at[half, which, u],
            device_id={"blk": even_b, "uly": owner},
        )

    def is_self(t):
        return jnp.logical_and(even, mine + t == u)

    def combine(half, which):
        wait_into(chip_in.at[half, which], c_recv.at[half, which])
        for t in range(4):
            total = stage[0, half, which, mine + t].astype(F32) + chip_in[half, which, t].astype(F32)
            stage[0, half, which, mine + t] = total.astype(BF16)

            @pl.when(jnp.logical_not(is_self(t)))
            def _():
                r1_copy(half, which, t).start()

    def r2_copy(part, which, j):
        peer = peers[j]
        return pltpu.make_async_remote_copy(
            src_ref=stage.at[1, part, which, peer],
            dst_ref=recv2.at[part, which, u],
            send_sem=r2_send.at[part, which, j],
            recv_sem=r2_recv.at[part, which, u],
            device_id={"blk": b, "uly": peer},
        )

    def send(part, which):
        for j in range(7):
            r2_copy(part, which, j).start()

    def run_step(step, carry):
        middle = jnp.logical_or(step == 1, step == 2)
        slot = jnp.where(even, step // 2, jnp.where(middle, 1, 0))
        part = jnp.where(even, lax.rem(step, 2), step // 2)

        for half in range(PARTS):
            @pl.when(step == jnp.where(even, 2 + half, 3 * half))
            def _():
                arrive_keys(half)

        acc[...] = jnp.zeros_like(acc)
        own = slot == core

        @pl.when(own)
        def _():
            value_sums(step, slot, part, True)

        @pl.when(jnp.logical_not(own))
        def _():
            value_sums(step, slot, part, False)

        def leave(which):
            put_pieces(stage.at[slot, part, which], acc[which])

            @pl.when(slot == 0)
            def _():
                chip_copy(part, which).start()

            @pl.when(slot == 1)
            def _():
                send(part, which)

        leave(1)

        @pl.when(step == 1)
        def _():
            combine(0, 1)
            combine(0, 0)

            @pl.when(far_receiver)
            def _():
                for half in range(2):
                    wait_into(quarter(1, half, ux), w_recv.at[half])
                    for dx in (1, 3, 2):
                        forward_copy(half, dx).start()

        key_sums(step, slot, part)
        leave(0)
        return carry

    lax.fori_loop(0, 4, run_step, 0)
    combine(1, 1)
    for head in range(HEADS):
        rows = slice(head % 2 * ROWS, (head % 2 + 1) * ROWS)
        dq_ref[:, head * DH : (head + 1) * DH] = (dq_acc[head // 2, rows] * SCALE).astype(BF16)

    combine(1, 0)

    def write(part, which, total):
        rows = slice(part * PIECE, (part + 1) * PIECE)
        turned = total.T
        if which == 0:
            turned = turned * SCALE
        dkv_ref[which, rows, :] = turned.astype(BF16)

    def finish_even(half, which):
        for sender in range(HEADS):
            local = jnp.logical_and(u == sender, u < 4)

            @pl.when(jnp.logical_not(local))
            def _():
                wait_into(recv1.at[half, which, sender], r1_recv.at[half, which, sender])

            @pl.when(local)
            def _():
                recv1[half, which, sender] = stage[0, half, which, sender]

        total = recv1[half, which, 0].astype(F32)
        for sender in range(1, HEADS):
            total = total + recv1[half, which, sender].astype(F32)
        write(half, which, total)

    @pl.when(even)
    def _():
        finish_even(0, 1)
        finish_even(0, 0)

    def z_copy(part, which):
        return pltpu.make_async_remote_copy(
            src_ref=zsend.at[part, which],
            dst_ref=zrecv.at[part, which],
            send_sem=z_send.at[part, which],
            recv_sem=z_recv.at[part, which],
            device_id={"blk": before, "uly": u},
        )

    steps = [(part, which) for part in range(PARTS) for which in (1, 0)]
    for part, which in steps:
        total = stage[1, part, which, u].astype(F32)
        for peer in peers:
            wait_into(recv2.at[part, which, peer], r2_recv.at[part, which, peer])
            total = total + recv2[part, which, peer].astype(F32)

        @pl.when(even)
        def _():
            zsend[part, which] = total.astype(BF16)
            z_copy(part, which).start()

        @pl.when(odd)
        def _():
            sums[part, which] = total

    @pl.when(even)
    def _():
        finish_even(1, 1)
        finish_even(1, 0)

    @pl.when(odd)
    def _():
        for part, which in steps:
            wait_into(zrecv.at[part, which], z_recv.at[part, which])
            write(part, which, sums[part, which] + zrecv[part, which].astype(F32))

    for j in range(7):
        norm_copy(j).wait_send()
        o_copy(j).wait_send()

    @pl.when(far_sender)
    def _():
        for half in range(2):
            far_copy(half).wait_send()

    @pl.when(jnp.logical_not(far_sender))
    def _():
        for part in range(PARTS):
            kv_copy(part).wait_send()

    @pl.when(far_receiver)
    def _():
        for half in range(2):
            for dx in (1, 3, 2):
                forward_copy(half, dx).wait_send()

    for half, which in steps:
        chip_copy(half, which).wait_send()
        for t in range(4):
            @pl.when(jnp.logical_not(is_self(t)))
            def _():
                r1_copy(half, which, t).wait_send()

    for part, which in steps:
        for j in range(7):
            r2_copy(part, which, j).wait_send()

        @pl.when(even)
        def _():
            z_copy(part, which).wait_send()


def hand_on(dq_in, dkv_in, dq_ref, dk_ref, dv_ref):
    dq_ref[...] = dq_in[...]
    dk_ref[...] = dkv_in[0]
    dv_ref[...] = dkv_in[1]


def body(query_rows, key_rows, value_rows, forward_output, grad_output, log_normalizer, block_order, block_table):
    vmem = pl.BlockSpec(memory_space=pltpu.VMEM)
    smem = pl.BlockSpec(memory_space=pltpu.SMEM)
    dma = pltpu.SemaphoreType.DMA
    piece = (DH, PIECE)
    scratch = [
        pltpu.VMEM((HEADS, ROWS, DH), BF16),
        pltpu.VMEM((HEADS, 1, ROWS), F32),
        pltpu.VMEM((2, PARTS, 2, HEADS, PIECE, DH), BF16),
        pltpu.VMEM((2, PARTS, 2 * DH, COLS), BF16),
        pltpu.VMEM((2, PARTS, 2 * DH, COLS), BF16),
        pltpu.VMEM((HEADS // 2, 2 * ROWS, 2 * DH), BF16),
        pltpu.VMEM((HEADS // 2, 2 * ROWS, 2 * DH), BF16),
        pltpu.VMEM((HEADS // 2, DH, 2 * ROWS), BF16),
        pltpu.VMEM((HEADS // 2, DH, 2 * ROWS), BF16),
        pltpu.VMEM((PARTS, ROWS, COLS), F32),
        pltpu.VMEM((HEADS // 2, 2 * ROWS, DH), F32),
        pltpu.VMEM((2, DH, COLS), F32),
        pltpu.VMEM((HEADS // 2, 2 * ROWS, COLS), F32),
        pltpu.VMEM((2, PARTS, 2, HEADS) + piece, BF16),
        pltpu.VMEM((PARTS, 2, 4) + piece, BF16),
        pltpu.VMEM((PARTS, 2, HEADS) + piece, BF16),
        pltpu.VMEM((PARTS, 2, HEADS) + piece, BF16),
        pltpu.VMEM((PARTS, 2) + piece, BF16),
        pltpu.VMEM((PARTS, 2) + piece, BF16),
        pltpu.VMEM((PARTS, 2) + piece, F32),
        dma((7,)), dma((HEADS,)),
        dma((7,)), dma((HEADS,)),
        dma((PARTS,)), dma((PARTS,)),
        dma((2,)), dma((2,)),
        dma((2, 4)), dma((2, 4)),
        dma((2, 2)), dma((2, 2)),
        dma((2, 2, 4)), dma((2, 2, HEADS)),
        dma((PARTS, 2, 7)), dma((PARTS, 2, HEADS)),
        dma((PARTS, 2)), dma((PARTS, 2)),
    ]
    dq, dkv = pl.pallas_call(
        kernel,
        out_shape=(
            jax.ShapeDtypeStruct((ROWS, HEADS * DH), BF16),
            jax.ShapeDtypeStruct((2, ROWS, DH), BF16),
        ),
        in_specs=[smem, smem] + [vmem] * 6,
        out_specs=(vmem, vmem),
        scratch_shapes=scratch,
        compiler_params=pltpu.CompilerParams(
            collective_id=0, has_side_effects=True, vmem_limit_bytes=56 << 20
        ),
        cost_estimate=pl.CostEstimate(
            flops=10 * ROWS * HEADS * 4096 * DH,
            bytes_accessed=5 << 20,
            transcendentals=ROWS * HEADS * 4096,
        ),
    )(
        block_order,
        block_table,
        query_rows,
        key_rows.reshape(HEADS, PARTS, PIECE, DH),
        value_rows.reshape(HEADS, PARTS, PIECE, DH),
        forward_output.reshape(HEADS, ROWS, DH),
        grad_output,
        log_normalizer.reshape(HEADS, 1, ROWS),
    )
    rows_out = jax.ShapeDtypeStruct((ROWS, DH), BF16)
    return pl.pallas_call(
        hand_on,
        out_shape=(jax.ShapeDtypeStruct((ROWS, HEADS * DH), BF16), rows_out, rows_out),
        in_specs=[vmem, vmem],
        out_specs=(vmem, vmem, vmem),
    )(dq, dkv)


def solution(mesh):
    in_specs = (
        P(("blk", "uly"), None),
        P("blk", None),
        P("blk", None),
        P("blk", "uly"),
        P(("blk", "uly"), None),
        P("uly", "blk"),
        P(),
        P(),
    )
    out_specs = (P(("blk", "uly"), None), P(("blk", "uly"), None), P(("blk", "uly"), None))
    return jax.shard_map(body, mesh=mesh, in_specs=in_specs, out_specs=out_specs, check_vma=False)
```

```python
import functools
import math

import jax
import jax.numpy as jnp
from jax import lax
from jax.experimental import pallas as pl
from jax.experimental.pallas import tpu as pltpu
from jax.sharding import PartitionSpec as P

BF16 = jnp.bfloat16
F32 = jnp.float32
BIG = 2.0**100
HEADS = 8
DH = 128
ROWS = 256
PIECE = 128
PARTS = 2
COLS = HEADS * PIECE
GROUPS = 32
PLANE = 16
SCALE = 1.0 / math.sqrt(DH)
EXP_SCALE = SCALE * math.log2(math.e)


def dot(a, b):
    return jnp.dot(a, b, preferred_element_type=F32)


def three_terms(column):
    high = column.astype(BF16)
    rest = column - high.astype(F32)
    middle = rest.astype(BF16)
    low = (rest - middle.astype(F32)).astype(BF16)
    return high.astype(F32), middle.astype(F32), low.astype(F32)


def extra_columns(column, lane):
    high, middle, low = three_terms(column)
    block = jnp.where(lane == 0, high, jnp.where(lane == 1, middle, jnp.where(lane == 2, low, 0.0)))
    return jnp.where(lane == 3, 1.0, block).astype(BF16)


def kernel(
    order_ref, table_ref, q_ref, k_ref, v_ref, o_ref, g_ref, norm_ref,
    dq_ref, dkv_ref,
    o_all, norm_all, kv_nat, k_aug, v_aug, q_aug, g_aug, q_t, g_t, mask_add,
    dq_acc, acc, probs_kept, stage1, stage2, chip_in, recv1, recv2, zsend, zrecv, sums,
    o_send, o_recv, n_send, n_recv, kv_send, kv_recv, w_send, w_recv, f_send, f_recv,
    c_send, c_recv, r1_send, r1_recv, r2_send, r2_recv, z_send, z_recv,
):
    b = lax.axis_index("blk")
    u = lax.axis_index("uly")
    core = lax.rem(b, 2)
    even = core == 0
    odd = core == 1
    even_b = b - core
    mate = b + 1 - 2 * core
    after = lax.rem(b + 1, GROUPS)
    before = lax.rem(b + GROUPS - 1, GROUPS)
    far_sender = lax.rem(b, PLANE) == PLANE - 1
    far_receiver = lax.rem(b, PLANE) == 0
    ux = u // 2
    uy = lax.rem(u, 2)
    peers = []
    for dx, dy in ((0, 1), (1, 0), (3, 0), (1, 1), (3, 1), (2, 0), (2, 1)):
        peers.append(lax.rem(ux + dx, 4) * 2 + lax.rem(uy + dy, 2))

    barrier = pltpu.get_barrier_semaphore()

    def greet(blk, uly):
        pl.semaphore_signal(barrier, inc=1, device_id={"blk": blk, "uly": uly})

    greet(mate, u)
    for peer in peers:
        greet(b, peer)
        greet(mate, peer)

    @pl.when(even)
    def _():
        greet(before, u)

    for part in range(PARTS):
        kv_nat[core, part, 0] = k_ref[:, part]
        kv_nat[core, part, 1] = v_ref[:, part]
    o_all[u] = o_ref[u]
    norm_all[u] = norm_ref[u]

    @pl.when(even)
    def _():
        pl.semaphore_wait(barrier, 15)

    @pl.when(odd)
    def _():
        pl.semaphore_wait(barrier, 16)

    def o_copies(j):
        peer = peers[j]
        copies = []
        for src, dst, send, recv in (
            (norm_ref, norm_all, n_send, n_recv),
            (o_ref, o_all, o_send, o_recv),
        ):
            copies.append(pltpu.make_async_remote_copy(
                src_ref=src.at[peer],
                dst_ref=dst.at[u],
                send_sem=send.at[j],
                recv_sem=recv.at[u],
                device_id={"blk": b, "uly": peer},
            ))
        return copies

    def kv_copy(part):
        return pltpu.make_async_remote_copy(
            src_ref=kv_nat.at[core, part],
            dst_ref=kv_nat.at[core, part],
            send_sem=kv_send.at[part],
            recv_sem=kv_recv.at[part],
            device_id={"blk": after, "uly": u},
        )

    def quarter(slot, half, x):
        return kv_nat.at[slot, half, :, pl.ds(2 * x, 2)]

    def far_copy(half):
        return pltpu.make_async_remote_copy(
            src_ref=quarter(core, half, ux),
            dst_ref=quarter(core, half, ux),
            send_sem=w_send.at[half],
            recv_sem=w_recv.at[half],
            device_id={"blk": after, "uly": u},
        )

    def forward_copy(half, dx):
        return pltpu.make_async_remote_copy(
            src_ref=quarter(1 - core, half, ux),
            dst_ref=quarter(1 - core, half, ux),
            send_sem=f_send.at[half, dx],
            recv_sem=f_recv.at[half, ux],
            device_id={"blk": b, "uly": lax.rem(ux + dx, 4) * 2 + uy},
        )

    @pl.when(far_sender)
    def _():
        for half in range(2):
            far_copy(half).start()

    @pl.when(jnp.logical_not(far_sender))
    def _():
        for part in range(PARTS):
            kv_copy(part).start()

    for j in range(7):
        for copy in o_copies(j):
            copy.start()

    own_half = u // 4
    q_seq = order_ref[2 * b + own_half]

    def blocked(k_seq):
        seen = jnp.logical_and(k_seq < q_seq, table_ref[q_seq, k_seq] == 1)
        return jnp.where(seen, 0.0, -BIG)

    other_add = blocked(order_ref[2 * b + 1 - own_half])
    before_add0 = blocked(order_ref[2 * before])
    before_add1 = blocked(order_ref[2 * before + 1])
    own_add0 = jnp.where(own_half == 0, 0.0, other_add)
    own_add1 = jnp.where(own_half == 0, other_add, 0.0)

    def build_keys(slot, part, add0, add1):
        sub = lax.broadcasted_iota(jnp.int32, (DH, COLS), 0)
        half_of = lax.broadcasted_iota(jnp.int32, (DH, COLS), 1) // (COLS // 2)
        k_aug[slot, part, 0:DH, :] = kv_nat[slot, part, 0].reshape(COLS, DH).T
        v_aug[slot, part, 0:DH, :] = kv_nat[slot, part, 1].reshape(COLS, DH).T
        minus = jnp.where(sub < 3, -1.0, 0.0)
        add = jnp.where(half_of == 0, add0, add1)
        k_aug[slot, part, DH : 2 * DH, :] = jnp.where(sub == 3, add, minus).astype(BF16)
        v_aug[slot, part, DH : 2 * DH, :] = minus.astype(BF16)

    def own_part(part, carry):
        build_keys(core, part, own_add0, own_add1)
        row = lax.broadcasted_iota(jnp.int32, (ROWS, COLS), 0) + u * ROWS
        col = lax.broadcasted_iota(jnp.int32, (ROWS, COLS), 1)
        key = (col // PIECE) * ROWS + part * PIECE + col % PIECE
        hidden = jnp.logical_and(col // (COLS // 2) == own_half, key > row)
        mask_add[part] = jnp.where(hidden, -BIG, 0.0)
        for which in range(2):
            acc[part, which] = jnp.zeros((DH, COLS), F32)
        return carry

    lax.fori_loop(0, PARTS, own_part, 0)
    for src, dst in ((q_ref, q_t), (g_ref, g_t)):
        turned = src[...].T
        for head in range(HEADS):
            cols = slice(head % 2 * ROWS, (head % 2 + 1) * ROWS)
            dst[head // 2, :, cols] = turned[head * DH : (head + 1) * DH]
    dq_acc[...] = jnp.zeros_like(dq_acc)

    def wait_into(dst, sem):
        pltpu.make_async_copy(dst, dst, sem).wait()

    def arrive_keys(half):
        slot = 1 - core

        @pl.when(far_receiver)
        def _():
            for dx in (1, 3, 2):
                x = lax.rem(ux + dx, 4)
                wait_into(quarter(slot, half, x), f_recv.at[half, x])

        @pl.when(jnp.logical_not(far_receiver))
        def _():
            wait_into(kv_nat.at[slot, half], kv_recv.at[half])

        build_keys(slot, half, before_add0, before_add1)

    lane = lax.broadcasted_iota(jnp.int32, (ROWS, DH), 1)

    def prepare(pair, member):
        head = 2 * pair + member

        @pl.when(head != u)
        def _():
            wait_into(norm_all.at[head], n_recv.at[head])
            wait_into(o_all.at[head], o_recv.at[head])

        cols = pl.ds(pl.multiple_of(head * DH, DH), DH)
        rows = slice(member * ROWS, (member + 1) * ROWS)
        q_head = q_ref[:, cols]
        g_head = g_ref[:, cols]
        norm = jnp.broadcast_to(norm_all[head], (DH, ROWS)).T / SCALE
        delta = jnp.sum(g_head.astype(F32) * o_all[head].astype(F32), axis=1, keepdims=True)
        q_aug[pair, rows, 0:DH] = q_head
        q_aug[pair, rows, DH : 2 * DH] = extra_columns(norm, lane)
        g_aug[pair, rows, 0:DH] = g_head
        g_aug[pair, rows, DH : 2 * DH] = extra_columns(delta, lane)

    def tile_probs(slot, part, pair, masked):
        scores = dot(q_aug[pair], k_aug[slot, part])
        if masked:
            scores = scores.reshape(2, ROWS, COLS) + mask_add[part][None]
            scores = scores.reshape(2 * ROWS, COLS)
        return jnp.exp2(scores * EXP_SCALE)

    def tile_keys(slot, part, pair, probs):
        grad_probs = dot(g_aug[pair], v_aug[slot, part])
        grad_scores = (probs * grad_probs).astype(BF16)
        dq_acc[pair] += dot(grad_scores, kv_nat[slot, part, 0].reshape(COLS, DH))
        return dot(q_t[pair], grad_scores)

    def tile_values(pair, probs):
        return dot(g_t[pair], probs.astype(BF16))

    def put_pieces(stage, total):
        for owner in range(HEADS):
            stage[owner] = total[:, owner * PIECE : (owner + 1) * PIECE].astype(BF16)

    def first_pairs(half, first, last, masked):
        def step(j, carry):
            pair = lax.rem(ux + j + (j // 2) * (1 - 2 * lax.rem(j, 2)), 4)
            if half == 0:
                prepare(pair, 0)
                prepare(pair, 1)
            probs = tile_probs(0, half, pair, masked)
            acc[half, 0] += tile_keys(0, half, pair, probs)
            acc[half, 1] += tile_values(pair, probs)
            return carry

        lax.fori_loop(first, last, step, 0)

    def first(half, first_pair, last_pair):
        @pl.when(even)
        def _():
            first_pairs(half, first_pair, last_pair, True)

        @pl.when(odd)
        def _():
            first_pairs(half, first_pair, last_pair, False)

    mine = 4 * core
    theirs = 4 - mine

    def chip_copy(half):
        return pltpu.make_async_remote_copy(
            src_ref=stage1.at[half, :, pl.ds(theirs, 4)],
            dst_ref=chip_in.at[half],
            send_sem=c_send.at[half],
            recv_sem=c_recv.at[half],
            device_id={"blk": mate, "uly": u},
        )

    def exchange(half):
        for which in range(2):
            put_pieces(stage1.at[half, which], acc[half, which])
        chip_copy(half).start()

    def r1_copy(half, t):
        owner = mine + t
        return pltpu.make_async_remote_copy(
            src_ref=stage1.at[half, :, owner],
            dst_ref=recv1.at[half, u],
            send_sem=r1_send.at[half, t],
            recv_sem=r1_recv.at[half, u],
            device_id={"blk": even_b, "uly": owner},
        )

    def is_self(t):
        return jnp.logical_and(even, mine + t == u)

    def combine(half):
        wait_into(chip_in.at[half], c_recv.at[half])
        for t in range(4):
            for which in range(2):
                total = stage1[half, which, mine + t].astype(F32) + chip_in[half, which, t].astype(F32)
                stage1[half, which, mine + t] = total.astype(BF16)

            @pl.when(jnp.logical_not(is_self(t)))
            def _():
                r1_copy(half, t).start()

    def r2_copy(part, which, j):
        peer = peers[j]
        return pltpu.make_async_remote_copy(
            src_ref=stage2.at[part, which, peer],
            dst_ref=recv2.at[part, which, u],
            send_sem=r2_send.at[part, which, j],
            recv_sem=r2_recv.at[part, which, u],
            device_id={"blk": b, "uly": peer},
        )

    def second_values(part, masked):
        total = None
        for pair in range(HEADS // 2):
            probs = tile_probs(1, part, pair, masked)
            probs_kept[pair] = probs
            term = tile_values(pair, probs)
            total = term if total is None else total + term
        put_pieces(stage2.at[part, 1], total)

    def second_keys(part):
        total = None
        for pair in range(HEADS // 2):
            term = tile_keys(1, part, pair, probs_kept[pair])
            total = term if total is None else total + term
        put_pieces(stage2.at[part, 0], total)

    @pl.when(odd)
    def _():
        arrive_keys(0)
        arrive_keys(1)

    first(0, 0, 4)
    exchange(0)
    first(1, 0, 1)
    combine(0)

    @pl.when(far_receiver)
    def _():
        for half in range(2):
            wait_into(quarter(1 - core, half, ux), w_recv.at[half])
            for dx in (1, 3, 2):
                forward_copy(half, dx).start()

    first(1, 1, 4)
    exchange(1)

    @pl.when(even)
    def _():
        arrive_keys(0)

    def second_step(part, carry):
        @pl.when(jnp.logical_and(even, part == 1))
        def _():
            arrive_keys(1)

        @pl.when(even)
        def _():
            second_values(part, False)

        @pl.when(odd)
        def _():
            second_values(part, True)

        @pl.when(part == 0)
        def _():
            combine(1)

        for j in reversed(range(7)):
            r2_copy(part, 1, j).start()
        second_keys(part)
        for j in reversed(range(7)):
            r2_copy(part, 0, j).start()
        return carry

    lax.fori_loop(0, PARTS, second_step, 0)

    for head in range(HEADS):
        rows = slice(head % 2 * ROWS, (head % 2 + 1) * ROWS)
        dq_ref[:, head * DH : (head + 1) * DH] = (dq_acc[head // 2, rows] * SCALE).astype(BF16)

    def write(part, which, total):
        rows = slice(part * PIECE, (part + 1) * PIECE)
        turned = total.T
        if which == 0:
            turned = turned * SCALE
        dkv_ref[which, rows, :] = turned.astype(BF16)

    @pl.when(even)
    def _():
        for half in range(2):
            for sender in range(HEADS):
                local = jnp.logical_and(u == sender, u < 4)

                @pl.when(jnp.logical_not(local))
                def _():
                    wait_into(recv1.at[half, sender], r1_recv.at[half, sender])

                @pl.when(local)
                def _():
                    for which in range(2):
                        recv1[half, sender, which] = stage1[half, which, sender]

            for which in range(2):
                total = recv1[half, 0, which].astype(F32)
                for sender in range(1, HEADS):
                    total = total + recv1[half, sender, which].astype(F32)
                write(half, which, total)

    def z_copy(part, which):
        return pltpu.make_async_remote_copy(
            src_ref=zsend.at[part, which],
            dst_ref=zrecv.at[part, which],
            send_sem=z_send.at[part, which],
            recv_sem=z_recv.at[part, which],
            device_id={"blk": before, "uly": u},
        )

    steps = [(part, which) for part in range(PARTS) for which in (1, 0)]
    for part, which in steps:
        total = stage2[part, which, u].astype(F32)
        for peer in peers:
            wait_into(recv2.at[part, which, peer], r2_recv.at[part, which, peer])
            total = total + recv2[part, which, peer].astype(F32)

        @pl.when(even)
        def _():
            zsend[part, which] = total.astype(BF16)
            z_copy(part, which).start()

        @pl.when(odd)
        def _():
            sums[part, which] = total

    @pl.when(odd)
    def _():
        for part, which in steps:
            wait_into(zrecv.at[part, which], z_recv.at[part, which])
            write(part, which, sums[part, which] + zrecv[part, which].astype(F32))

    for j in range(7):
        for copy in o_copies(j):
            copy.wait_send()

    @pl.when(far_sender)
    def _():
        for half in range(2):
            far_copy(half).wait_send()

    @pl.when(jnp.logical_not(far_sender))
    def _():
        for part in range(PARTS):
            kv_copy(part).wait_send()

    @pl.when(far_receiver)
    def _():
        for half in range(2):
            for dx in (1, 3, 2):
                forward_copy(half, dx).wait_send()

    for half in range(2):
        chip_copy(half).wait_send()
        for t in range(4):
            @pl.when(jnp.logical_not(is_self(t)))
            def _():
                r1_copy(half, t).wait_send()

    for part, which in steps:
        for j in range(7):
            r2_copy(part, which, j).wait_send()

        @pl.when(even)
        def _():
            z_copy(part, which).wait_send()


def hand_on(dq_in, dkv_in, dq_ref, dk_ref, dv_ref):
    dq_ref[...] = dq_in[...]
    dk_ref[...] = dkv_in[0]
    dv_ref[...] = dkv_in[1]


def body(query_rows, key_rows, value_rows, forward_output, grad_output, log_normalizer, block_order, block_table):
    vmem = pl.BlockSpec(memory_space=pltpu.VMEM)
    smem = pl.BlockSpec(memory_space=pltpu.SMEM)
    dma = pltpu.SemaphoreType.DMA
    piece = (DH, PIECE)
    scratch = [
        pltpu.VMEM((HEADS, ROWS, DH), BF16),
        pltpu.VMEM((HEADS, 1, ROWS), F32),
        pltpu.VMEM((2, PARTS, 2, HEADS, PIECE, DH), BF16),
        pltpu.VMEM((2, PARTS, 2 * DH, COLS), BF16),
        pltpu.VMEM((2, PARTS, 2 * DH, COLS), BF16),
        pltpu.VMEM((HEADS // 2, 2 * ROWS, 2 * DH), BF16),
        pltpu.VMEM((HEADS // 2, 2 * ROWS, 2 * DH), BF16),
        pltpu.VMEM((HEADS // 2, DH, 2 * ROWS), BF16),
        pltpu.VMEM((HEADS // 2, DH, 2 * ROWS), BF16),
        pltpu.VMEM((PARTS, ROWS, COLS), F32),
        pltpu.VMEM((HEADS // 2, 2 * ROWS, DH), F32),
        pltpu.VMEM((PARTS, 2, DH, COLS), F32),
        pltpu.VMEM((HEADS // 2, 2 * ROWS, COLS), F32),
        pltpu.VMEM((PARTS, 2, HEADS) + piece, BF16),
        pltpu.VMEM((PARTS, 2, HEADS) + piece, BF16),
        pltpu.VMEM((PARTS, 2, 4) + piece, BF16),
        pltpu.VMEM((PARTS, HEADS, 2) + piece, BF16),
        pltpu.VMEM((PARTS, 2, HEADS) + piece, BF16),
        pltpu.VMEM((PARTS, 2) + piece, BF16),
        pltpu.VMEM((PARTS, 2) + piece, BF16),
        pltpu.VMEM((PARTS, 2) + piece, F32),
        dma((7,)), dma((HEADS,)),
        dma((7,)), dma((HEADS,)),
        dma((PARTS,)), dma((PARTS,)),
        dma((2,)), dma((2,)),
        dma((2, 4)), dma((2, 4)),
        dma((2,)), dma((2,)),
        dma((2, 4)), dma((2, HEADS)),
        dma((PARTS, 2, 7)), dma((PARTS, 2, HEADS)),
        dma((PARTS, 2)), dma((PARTS, 2)),
    ]
    dq, dkv = pl.pallas_call(
        kernel,
        out_shape=(
            jax.ShapeDtypeStruct((ROWS, HEADS * DH), BF16),
            jax.ShapeDtypeStruct((2, ROWS, DH), BF16),
        ),
        in_specs=[smem, smem] + [vmem] * 6,
        out_specs=(vmem, vmem),
        scratch_shapes=scratch,
        compiler_params=pltpu.CompilerParams(
            collective_id=0, has_side_effects=True, vmem_limit_bytes=56 << 20
        ),
        cost_estimate=pl.CostEstimate(
            flops=10 * ROWS * HEADS * 4096 * DH,
            bytes_accessed=5 << 20,
            transcendentals=ROWS * HEADS * 4096,
        ),
    )(
        block_order,
        block_table,
        query_rows,
        key_rows.reshape(HEADS, PARTS, PIECE, DH),
        value_rows.reshape(HEADS, PARTS, PIECE, DH),
        forward_output.reshape(HEADS, ROWS, DH),
        grad_output,
        log_normalizer.reshape(HEADS, 1, ROWS),
    )
    rows_out = jax.ShapeDtypeStruct((ROWS, DH), BF16)
    return pl.pallas_call(
        hand_on,
        out_shape=(jax.ShapeDtypeStruct((ROWS, HEADS * DH), BF16), rows_out, rows_out),
        in_specs=[vmem, vmem],
        out_specs=(vmem, vmem, vmem),
    )(dq, dkv)


def solution(mesh):
    in_specs = (
        P(("blk", "uly"), None),
        P("blk", None),
        P("blk", None),
        P("blk", "uly"),
        P(("blk", "uly"), None),
        P("uly", "blk"),
        P(),
        P(),
    )
    out_specs = (P(("blk", "uly"), None), P(("blk", "uly"), None), P(("blk", "uly"), None))
    return jax.shard_map(body, mesh=mesh, in_specs=in_specs, out_specs=out_specs, check_vma=False)
```
